32 devices in a mesh: pipe: 8 (over z, core), expert: 4 (over y, x).
Axes of the slice: x: 2, y: 2, z: 4, core: 2. Of those that a mesh axis runs over, the one named last changes fastest.
Arguments:
- fwd_in: bfloat16 [8, 256, 3584], P('pipe', 'expert'), may hold values from -6 to 6
- bwd_in: bfloat16 [8, 256, 3584], P('pipe', 'expert'), may hold values from -6 to 6
- bwd_grad_in: bfloat16 [8, 256, 3584], P('pipe', 'expert'), may hold values from -6 to 6
- w_gate: bfloat16 [8, 7168, 1024], P('pipe', 'expert'), may hold values from -0.09375 to 0.09375
- w_up: bfloat16 [8, 7168, 1024], P('pipe', 'expert'), may hold values from -0.09375 to 0.09375
- w_down: bfloat16 [8, 1024, 7168], P('pipe', None, 'expert'), may hold values from -0.1875 to 0.1875
- fwd_ids: int32 [8, 256, 1], P('pipe', 'expert'), may hold values from 0 to 1; in each aligned block of 64 rows (0 to 63, 64 to 127, ..., all dimensions but the last counted through in order) at most 40 rows name the same one
- fwd_gates: float32 [8, 256, 1], P('pipe', 'expert'), may hold values from 0.25 to 1
- bwd_ids: int32 [8, 256, 1], P('pipe', 'expert'), may hold values from 0 to 1; in each aligned block of 64 rows (0 to 63, 64 to 127, ..., all dimensions but the last counted through in order) at most 40 rows name the same one
- bwd_gates: float32 [8, 256, 1], P('pipe', 'expert'), may hold values from 0.25 to 1
Outputs:
- fwd_out: bfloat16 [8, 256, 3584], P('pipe', 'expert')
- bwd_out: bfloat16 [8, 256, 3584], P('pipe', 'expert')
The draws below stay inside these ranges and needn't reach their ends.
Inputs may be any that keep to these rules, and one draw needn't show every extreme that they name: `fwd_ids`: each row names 1 different experts; among the 64 tokens of one device (aligned blocks of rows) no expert is named more than 40 times. `bwd_ids`: each row names 1 different experts; among the 64 tokens of one device (aligned blocks of rows) no expert is named more than 40 times.
All inputs are finite; a program needn't handle non-finite values.
Results may differ from the reference program's by a relative error of at most 0.01.
Values may be sent and summed in bfloat16 or wider, within the bound.
No kernel may reach another device: no remote copies, remote signals or barrier semaphores. Data moves between devices by JAX's collectives and lax.ppermute only.
A program may use at most 128 MiB of HBM per device.

```python
import math
import jax
import jax.numpy as jnp
import numpy as np
from jax import lax

D = 3584
FF = 1024
EXPERTS = 2
TOP = 1
TOK_DEV = 64
CAP = 40
GROUP = 2
SECTIONS = 8
TOKENS = 256


def shard_levels(own_key, dims, split, least, largest):
    level = 1.0
    for position, blocks in split:
        draws = jax.random.uniform(jax.random.fold_in(jax.random.fold_in(own_key, 6), position), (blocks,), jnp.float32, least / len(split), largest / len(split))
        level = level * jnp.repeat(jnp.exp(draws), dims[position] // blocks).reshape((-1,) + (1,) * (len(dims) - 1 - position))
    return level


def assign_block(rng, own, number, rows, number_of, top, most, skew):
    order = jax.random.permutation(rng, number_of)
    crowded, usual = portions_of(number_of, rows * top, most, skew, True), portions_of(number_of, rows * top, most, skew, False)
    places = jnp.arange(number_of)

    def named(tallies, offset_by):
        used = int((tallies > 0).sum())
        fixed = max(1, used // 4)
        passed = fixed + (places - fixed + offset_by * (used - fixed)) % max(1, number_of - fixed)
        return jnp.zeros((number_of,), jnp.int32).at[order[jnp.where(places < fixed, places, passed)]].set(jnp.asarray(tallies, jnp.int32))

    tallies = jnp.where(number % 4 == 0, named(crowded, number // 4), named(usual, number - number // 4 - 1))
    mixed = jax.random.permutation(jax.random.fold_in(own, 3), number_of)
    source_of, receiver = mixed[0:number_of // 2 * 2:2], mixed[1:number_of // 2 * 2:2]
    margin = jnp.minimum(tallies[source_of] - 1, most - tallies[receiver]) // 2
    margin = jnp.where((source_of == order[0]) | (receiver == order[0]) | (tallies[receiver] == 0), 0, jnp.maximum(margin, 0))
    passed = jax.random.randint(jax.random.fold_in(own, 4), (number_of // 2,), 0, 1 << 20) % (margin + 1)
    tallies = tallies.at[source_of].add(-passed).at[receiver].add(passed)
    members = jnp.searchsorted(jnp.cumsum(tallies), jnp.arange(rows * top), side="right").astype(jnp.int32)
    grid = members.reshape(top, rows).T
    grid = grid[jax.random.permutation(jax.random.fold_in(own, 1), rows)]
    offset_by = jax.random.randint(jax.random.fold_in(own, 2), (rows, 1), 0, top)
    return jnp.take_along_axis(grid, (jnp.arange(top)[None, :] + offset_by) % top, axis=1)


def portions_of(count, total, most, skew, full):
    loads = [(1 << 20) // math.isqrt(grade ** skew) + 1 for grade in range(1, count + 1)]
    largest = most if full else min(most, max(-(-total // count), total * loads[0] // sum(loads)))
    least = 1 if total - largest >= count - 1 else 0
    holding, surplus = [largest] + [least] * (count - 1), total - largest - least * (count - 1)
    while surplus > 0:
        candidates = [i for i in range(1, count) if holding[i] < largest] or [i for i in range(1, count) if holding[i] < most]
        mass, remaining = sum([loads[i] for i in candidates]), surplus
        for i in candidates:
            addition = min(most - holding[i], max(1, remaining * loads[i] // mass), surplus)
            holding[i] = holding[i] + addition
            surplus = surplus - addition
    return np.array(holding)


def noise(stream_key, extent, scale, limit, shards=(), kind=jnp.bfloat16):
    result = scale * jax.random.normal(stream_key, extent, jnp.float32)
    if shards:
        result = result * shard_levels(stream_key, extent, shards, -0.22, 0.18)
    return jnp.clip(result, -limit, limit).astype(kind)


def setup_inputs(seed: int = 0) -> dict:
    key_list = jax.random.split(jax.random.key(seed), 11)
    fwd_in = noise(key_list[0], (SECTIONS, TOKENS, D), 1.0, 6.0, ((0, 8), (1, 4)))
    bwd_in = noise(key_list[1], (SECTIONS, TOKENS, D), 1.0, 6.0, ((0, 8), (1, 4)))
    bwd_grad_in = noise(key_list[2], (SECTIONS, TOKENS, D), 1.0, 6.0, ((0, 8), (1, 4)))
    w_gate = noise(key_list[3], (SECTIONS, EXPERTS * D, FF), D ** -0.5, 0.09375, ((0, 8), (1, 4)))
    w_up = noise(key_list[4], (SECTIONS, EXPERTS * D, FF), D ** -0.5, 0.09375, ((0, 8), (1, 4)))
    w_down = noise(key_list[5], (SECTIONS, FF, EXPERTS * D), FF ** -0.5, 0.1875, ((0, 8), (2, 4)))
    fwd_ids_keys = jax.random.split(jax.random.fold_in(key_list[6], 1), SECTIONS * TOKENS // TOK_DEV)
    fwd_ids_turns = jax.random.permutation(jax.random.fold_in(key_list[6], 3), SECTIONS * TOKENS // TOK_DEV)
    fwd_ids = jax.vmap(lambda own, number: assign_block(jax.random.fold_in(key_list[6], 2), own, number, TOK_DEV, EXPERTS, TOP, CAP, 1))(fwd_ids_keys, fwd_ids_turns).reshape((SECTIONS, TOKENS, TOP))
    fwd_gates = jnp.clip(0.25 + 0.75 * jax.random.uniform(key_list[7], (SECTIONS, TOKENS, TOP), jnp.float32) ** shard_levels(key_list[7], (SECTIONS, TOKENS, TOP), ((0, 8), (1, 4)), -0.2, 0.2), 0.25, 1.0)
    bwd_ids_keys = jax.random.split(jax.random.fold_in(key_list[8], 1), SECTIONS * TOKENS // TOK_DEV)
    bwd_ids_turns = jax.random.permutation(jax.random.fold_in(key_list[8], 3), SECTIONS * TOKENS // TOK_DEV)
    bwd_ids = jax.vmap(lambda own, number: assign_block(jax.random.fold_in(key_list[8], 2), own, number, TOK_DEV, EXPERTS, TOP, CAP, 1))(bwd_ids_keys, bwd_ids_turns).reshape((SECTIONS, TOKENS, TOP))
    bwd_gates = jnp.clip(0.25 + 0.75 * jax.random.uniform(key_list[9], (SECTIONS, TOKENS, TOP), jnp.float32) ** shard_levels(key_list[9], (SECTIONS, TOKENS, TOP), ((0, 8), (1, 4)), -0.2, 0.2), 0.25, 1.0)
    return {"fwd_in": fwd_in, "bwd_in": bwd_in, "bwd_grad_in": bwd_grad_in, "w_gate": w_gate, "w_up": w_up, "w_down": w_down, "fwd_ids": fwd_ids, "fwd_gates": fwd_gates, "bwd_ids": bwd_ids, "bwd_gates": bwd_gates}


def slice_sum(rows, mats):
    token_count = rows.shape[0]
    width = rows.shape[1] // GROUP
    pieces = rows.reshape(token_count, GROUP, width).astype(jnp.float32)
    blocks = mats.reshape(GROUP, width, mats.shape[1]).astype(jnp.float32)
    partial_value = jnp.einsum("tgk,gkc->gtc", pieces, blocks).astype(jnp.bfloat16)
    return jnp.sum(partial_value.astype(jnp.float32), axis=0)


def forward_section(inputs, expert_ids, gate_values, gate_all, up_all, down_all):
    def one_expert(total, expert):
        joined = jnp.concatenate([gate_all[expert], up_all[expert]], axis=1)
        summed = slice_sum(inputs, joined)
        hidden = (jax.nn.silu(summed[:, :FF]) * summed[:, FF:]).astype(jnp.bfloat16)
        expert_out = jnp.dot(hidden, down_all[expert], preferred_element_type=jnp.float32).astype(jnp.bfloat16)
        weight = jnp.sum(jnp.where(expert_ids == expert, gate_values, 0.0), axis=1)
        return total + weight[:, None] * expert_out.astype(jnp.float32), None

    start = jnp.zeros(inputs.shape, jnp.float32)
    total, unused = lax.scan(one_expert, start, jnp.arange(EXPERTS, dtype=jnp.int32))
    return (inputs.astype(jnp.float32) + total).astype(jnp.bfloat16)


def backward_section(inputs, grads, expert_ids, gate_values, gate_all, up_all, down_all):
    def one_expert(total, expert):
        gate_mat = gate_all[expert]
        up_mat = up_all[expert]
        joined = jnp.concatenate([gate_mat, up_mat], axis=1)
        summed = slice_sum(inputs, joined)
        back_gate = summed[:, :FF]
        back_up = summed[:, FF:]
        grad_hidden = slice_sum(grads, down_all[expert].T)
        sig_gate = jax.nn.sigmoid(back_gate)
        grad_gate = (grad_hidden * back_up * sig_gate * (1.0 + back_gate * (1.0 - sig_gate))).astype(jnp.bfloat16)
        grad_up = (grad_hidden * jax.nn.silu(back_gate)).astype(jnp.bfloat16)
        expert_grad = jnp.dot(grad_gate, gate_mat.T, preferred_element_type=jnp.float32)
        expert_grad = expert_grad + jnp.dot(grad_up, up_mat.T, preferred_element_type=jnp.float32)
        expert_grad = expert_grad.astype(jnp.bfloat16)
        weight = jnp.sum(jnp.where(expert_ids == expert, gate_values, 0.0), axis=1)
        return total + weight[:, None] * expert_grad.astype(jnp.float32), None

    start = jnp.zeros(inputs.shape, jnp.float32)
    total, unused = lax.scan(one_expert, start, jnp.arange(EXPERTS, dtype=jnp.int32))
    return (grads.astype(jnp.float32) + total).astype(jnp.bfloat16)


def reference(fwd_in, bwd_in, bwd_grad_in, w_gate, w_up, w_down, fwd_ids, fwd_gates, bwd_ids, bwd_gates):
    section_x = jnp.concatenate([fwd_in[:1], fwd_in[:-1]], axis=0)
    section_g = jnp.concatenate([bwd_grad_in[1:], bwd_grad_in[-1:]], axis=0)
    gate_all = w_gate.reshape(SECTIONS, EXPERTS, D, FF)
    up_all = w_up.reshape(SECTIONS, EXPERTS, D, FF)
    down_all = jnp.transpose(w_down.reshape(SECTIONS, FF, EXPERTS, D), (0, 2, 1, 3))

    def per_section(items):
        inputs, saved, grads, gate_mats, up_mats, down_mats, f_ids, f_gates, b_ids, b_gates = items
        forward_out = forward_section(inputs, f_ids, f_gates, gate_mats, up_mats, down_mats)
        backward_out = backward_section(saved, grads, b_ids, b_gates, gate_mats, up_mats, down_mats)
        return forward_out, backward_out

    fwd_out, bwd_out = lax.map(per_section, (section_x, bwd_in, section_g, gate_all, up_all, down_all, fwd_ids, fwd_gates, bwd_ids, bwd_gates))
    return fwd_out, bwd_out
```

```python
import functools

import jax
import jax.numpy as jnp
from jax import lax
from jax.experimental import pallas as pl
from jax.experimental.pallas import tpu as pltpu
from jax.sharding import PartitionSpec as P

EXPERTS = 2
CAP = 40
BF16 = jnp.bfloat16
F32 = jnp.float32
VMEM_LIMIT = 40 * 1024 * 1024


def kernel_call(kernel, out_shape, grid, in_specs, out_specs, flops, moved):
    return pl.pallas_call(
        kernel,
        out_shape=out_shape,
        grid=grid,
        in_specs=in_specs,
        out_specs=out_specs,
        compiler_params=pltpu.CompilerParams(vmem_limit_bytes=VMEM_LIMIT),
        cost_estimate=pl.CostEstimate(flops=flops, bytes_accessed=moved, transcendentals=0),
    )


def full(shape):
    return pl.BlockSpec(shape, lambda j: (0,) * len(shape))


def tables(ids_row, expert, dtype):
    tokens = ids_row.shape[1]
    row = lax.broadcasted_iota(jnp.int32, (tokens, tokens), 0)
    col = lax.broadcasted_iota(jnp.int32, (tokens, tokens), 1)
    earlier = (row < col).astype(BF16)
    mine = jnp.broadcast_to(ids_row == expert, (8, tokens))
    before = jnp.dot(mine.astype(BF16), earlier, preferred_element_type=F32)[:1].astype(jnp.int32)
    place = lax.broadcasted_iota(jnp.int32, (1, tokens), 1)
    slot = lax.broadcasted_iota(jnp.int32, (CAP, tokens), 0)
    same = ids_row == expert
    table_same = ((slot == before) & same).astype(dtype)
    table_other = ((slot == place - before) & jnp.logical_not(same)).astype(dtype)
    return table_same, table_other


def slot_kernel(group, *refs):
    ids_ref, *rest = refs
    xs, (same_ref, other_ref) = rest[:group], rest[group:]
    expert = lax.axis_index("expert") // group
    same_rows, other_rows = [], []
    for r in range(group):
        t_same, t_other = tables(ids_ref[r : r + 1, :], expert, BF16)
        both = jnp.concatenate([t_same, t_other], axis=0)
        rows = jnp.dot(both, xs[r][...], preferred_element_type=F32)
        same_rows.append(rows[:CAP])
        other_rows.append(rows[CAP:])
    same_ref[...] = jnp.concatenate(same_rows, axis=0).astype(BF16)
    other_ref[...] = jnp.concatenate(other_rows, axis=0).astype(BF16)


def slot_rows(ids, xs):
    group = len(xs)
    tokens, width = xs[0].shape
    out = jax.ShapeDtypeStruct((group * CAP, width), BF16)
    return kernel_call(
        functools.partial(slot_kernel, group),
        (out, out),
        (1,),
        [full(ids.shape)] + [full(x.shape) for x in xs],
        (full(out.shape), full(out.shape)),
        2 * group * 2 * CAP * tokens * width,
        2 * group * (tokens + 2 * CAP) * width,
    )(ids, *xs)


def split_rows(acc, parts, group, outs, put):
    for r in range(group):
        rows = [acc[(p * group + r) * CAP : (p * group + r + 1) * CAP] for p in range(parts)]
        put(outs[r], jnp.concatenate(rows, axis=0).astype(BF16))


def dot_nt(a, b):
    return lax.dot_general(a, b, (((1,), (1,)), ((), ())), preferred_element_type=F32)


def in_kernel(parts, group, *refs):
    rows = jnp.concatenate([refs[p][...] for p in range(parts)], axis=0)
    gate, up, *outs = refs[parts:]
    for k, mat in enumerate((gate, up)):

        def put(ref, value, k=k):
            ref[k] = value

        split_rows(
            jnp.dot(rows, mat[...], preferred_element_type=F32), parts, group, outs, put
        )


def in_partials(parts, gate, up, group):
    width, hidden = gate.shape
    tile = 256
    rows = len(parts) * CAP
    out = jax.ShapeDtypeStruct((2, rows, hidden), BF16)
    column = pl.BlockSpec((width, tile), lambda j: (0, j))
    return kernel_call(
        functools.partial(in_kernel, len(parts), group),
        (out,) * group,
        (hidden // tile,),
        [full(p.shape) for p in parts] + [column, column],
        (pl.BlockSpec((2, rows, tile), lambda j: (0, 0, j)),) * group,
        2 * rows * group * width * 2 * hidden,
        2 * 2 * width * hidden,
    )(*parts, gate, up)


def grad_kernel(parts, group, *refs):
    rows = jnp.concatenate([refs[p][...] for p in range(parts)], axis=0)
    down, *outs = refs[parts:]

    def put(ref, value):
        ref[...] = value

    split_rows(dot_nt(rows, down[...]), parts, group, outs, put)


def grad_partials(parts, down, group):
    hidden, width = down.shape
    tile = 256
    rows = len(parts) * CAP
    out = jax.ShapeDtypeStruct((rows, hidden), BF16)
    return kernel_call(
        functools.partial(grad_kernel, len(parts), group),
        (out,) * group,
        (hidden // tile,),
        [full(p.shape) for p in parts] + [pl.BlockSpec((tile, width), lambda j: (j, 0))],
        (pl.BlockSpec((rows, tile), lambda j: (0, j)),) * group,
        2 * rows * group * width * hidden,
        2 * width * hidden,
    )(*parts, down)


def width_tile(width):
    return 256 if width % 256 == 0 else width


def down_kernel(group, *refs):
    hs, (down, *outs) = refs[:group], refs[group:]
    rows = jnp.concatenate([h[...] for h in hs], axis=0)
    acc = jnp.dot(rows, down[...], preferred_element_type=F32).astype(BF16)
    for p in range(2):
        for r in range(group):
            at = (r * 2 + p) * CAP
            outs[p * group + r][...] = acc[at : at + CAP]


def down_rows(hs, down):
    group = len(hs)
    hidden, width = down.shape
    tile = width_tile(width)
    out = jax.ShapeDtypeStruct((CAP, width), BF16)
    return kernel_call(
        functools.partial(down_kernel, group),
        (out,) * (2 * group),
        (width // tile,),
        [full(h.shape) for h in hs] + [pl.BlockSpec((hidden, tile), lambda j: (0, j))],
        (pl.BlockSpec((CAP, tile), lambda j: (0, j)),) * (2 * group),
        2 * group * 2 * CAP * hidden * width,
        2 * hidden * width,
    )(*hs, down)


def back_kernel(group, *refs):
    gs, (gate, up, *outs) = refs[:group], refs[group:]
    grads_gate = jnp.concatenate([g[0] for g in gs], axis=0)
    grads_up = jnp.concatenate([g[1] for g in gs], axis=0)
    acc = (dot_nt(grads_gate, gate[...]) + dot_nt(grads_up, up[...])).astype(BF16)
    for p in range(2):
        for r in range(group):
            at = (r * 2 + p) * CAP
            outs[p * group + r][...] = acc[at : at + CAP]


def back_rows(gs, gate, up):
    group = len(gs)
    width, hidden = gate.shape
    tile = width_tile(width)
    out = jax.ShapeDtypeStruct((CAP, width), BF16)
    row = pl.BlockSpec((tile, hidden), lambda j: (j, 0))
    return kernel_call(
        functools.partial(back_kernel, group),
        (out,) * (2 * group),
        (width // tile,),
        [full(g.shape) for g in gs] + [row, row],
        (pl.BlockSpec((CAP, tile), lambda j: (0, j)),) * (2 * group),
        2 * group * 2 * CAP * hidden * 2 * width,
        2 * 2 * hidden * width,
    )(*gs, gate, up)


def combine_kernel(group, *refs):
    ids, gates, base, *rest = refs
    same, other, out = rest[:group], rest[group : 2 * group], rest[2 * group]
    index = lax.axis_index("expert")
    t_same, t_other = tables(ids[...], index // group, BF16)
    tokens = base.shape[0]
    width = same[0].shape[1]
    row = lax.broadcasted_iota(jnp.int32, (tokens, tokens), 0)
    col = lax.broadcasted_iota(jnp.int32, (tokens, tokens), 1)
    weight = jnp.sum(jnp.where(row == col, gates[...], 0.0), axis=1, keepdims=True)
    contract = (((0,), (0,)), ((), ()))
    table = jnp.concatenate([t_same, t_other], axis=0)
    for r in range(group):
        blocks = jnp.concatenate([same[r][...], other[r][...]], axis=0)
        picked = lax.dot_general(table, blocks, contract, preferred_element_type=F32)
        for own in range(group):

            @pl.when(lax.rem(index, group) == own)
            def _(own=own, r=r, picked=picked):
                at = (own ^ r) * width
                out[:, at : at + width] = (
                    base[:, at : at + width].astype(F32) + weight * picked
                ).astype(BF16)


def combine(ids, gates, base, same, other):
    group = len(same)
    return kernel_call(
        functools.partial(combine_kernel, group),
        jax.ShapeDtypeStruct(base.shape, BF16),
        (1,),
        [full(v.shape) for v in (ids, gates, base, *same, *other)],
        full(base.shape),
        4 * CAP * base.shape[0] * base.shape[1],
        8 * base.shape[0] * base.shape[1],
    )(ids, gates, base, *same, *other)


def body(fwd_in, bwd_in, bwd_grad_in, w_gate, w_up, w_down, fwd_ids, fwd_gates, bwd_ids, bwd_gates):
    sections = lax.axis_size("pipe")
    devices = lax.axis_size("expert")
    group = devices // EXPERTS
    partners = range(1, group)
    section = lax.axis_index("pipe")
    slice_index = lax.rem(lax.axis_index("expert"), group)
    tokens, model = fwd_in.shape[1:]
    width = model // group
    gate, up, down = w_gate[0], w_up[0], w_down[0]

    def to_partner(value, mask):
        return lax.ppermute(value, "expert", [(i, i ^ mask) for i in range(devices)])

    def along(value, pairs):
        flat = [(a * devices + i, b * devices + j) for (a, i), (b, j) in pairs]
        return lax.ppermute(value, ("pipe", "expert"), flat)

    def piece(value, r):
        return lax.dynamic_slice_in_dim(value, (slice_index ^ r) * width, width, axis=1)

    first, last = 0, sections - 1
    fwd_in, bwd_in, bwd_grad_in = fwd_in[0], bwd_in[0], bwd_grad_in[0]
    own_ids = jnp.concatenate([fwd_ids.reshape(1, tokens), bwd_ids.reshape(1, tokens)], axis=0)
    all_ids = [own_ids] + [to_partner(own_ids, r) for r in partners]
    ids_fwd = jnp.concatenate([v[:1] for v in all_ids], axis=0)
    ids_bwd = jnp.concatenate([v[1:] for v in all_ids], axis=0)

    saved = [piece(bwd_in, 0)] + [to_partner(piece(bwd_in, r), r) for r in partners]
    steps = [(p, p + 1) for p in range(last)]
    x_here = lax.ppermute(fwd_in, "pipe", steps)
    g_here = lax.ppermute(bwd_grad_in, "pipe", [(b, a) for a, b in steps])
    section_x = jnp.where(section == first, fwd_in, x_here)
    section_g = jnp.where(section == last, bwd_grad_in, g_here)
    xs, gs = [piece(section_x, 0)], [piece(section_g, 0)]
    for r in partners:
        x_piece, g_piece = piece(fwd_in, r), piece(bwd_grad_in, r)
        x_far = along(
            x_piece, [((a, i), (b, i ^ r)) for a, b in steps for i in range(devices)]
        )
        g_far = along(
            g_piece, [((b, i), (a, i ^ r)) for a, b in steps for i in range(devices)]
        )
        kept = along(
            jnp.where(section == first, x_piece, g_piece),
            [((p, i), (p, i ^ r)) for p in (first, last) for i in range(devices)],
        )
        xs.append(jnp.where(section == first, kept, x_far))
        gs.append(jnp.where(section == last, kept, g_far))

    def dispatch(ids, pieces):
        same, other = slot_rows(ids, pieces)
        return same, to_partner(other, group)

    saved_same, saved_other = dispatch(ids_bwd, saved)
    x_same, x_other = dispatch(ids_fwd, xs)
    g_same, g_other = dispatch(ids_bwd, gs)

    def summed(partials):
        total = partials[0].astype(F32)
        for r in partners:
            total = total + to_partner(partials[r], r).astype(F32)
        return total

    back = summed(in_partials([saved_same, saved_other], gate, up, group))
    ahead = summed(in_partials([x_same, x_other], gate, up, group))
    grad_hidden = summed(grad_partials([g_same, g_other], down, group))

    hidden = (jax.nn.silu(ahead[0]) * ahead[1]).astype(BF16)
    hiddens = [hidden] + [to_partner(hidden, r) for r in partners]
    sig = jax.nn.sigmoid(back[0])
    grad_gate = grad_hidden * back[1] * sig * (1.0 + back[0] * (1.0 - sig))
    grad_up = grad_hidden * (back[0] * sig)
    grads = jnp.stack([grad_gate.astype(BF16), grad_up.astype(BF16)])
    all_grads = [grads] + [to_partner(grads, r) for r in partners]

    def returned(blocks):
        same = [blocks[0]] + [to_partner(blocks[r], r) for r in partners]
        other = [to_partner(blocks[group + r], group + r) for r in range(group)]
        return same, other

    fwd_same, fwd_other = returned(down_rows(hiddens, down))
    bwd_same, bwd_other = returned(back_rows(all_grads, gate, up))
    fwd_out = combine(
        ids_fwd[:1], fwd_gates.reshape(1, tokens), section_x, fwd_same, fwd_other
    )
    bwd_out = combine(
        ids_bwd[:1], bwd_gates.reshape(1, tokens), section_g, bwd_same, bwd_other
    )
    return (fwd_out[None], bwd_out[None])


def solution(mesh):
    spec = P("pipe", "expert", None)
    return jax.shard_map(
        body,
        mesh=mesh,
        in_specs=(spec,) * 5 + (P("pipe", None, "expert"),) + (spec,) * 4,
        out_specs=(spec, spec),
        check_vma=False,
    )
```

```python
import functools

import jax
import jax.numpy as jnp
from jax import lax
from jax.experimental import pallas as pl
from jax.experimental.pallas import tpu as pltpu
from jax.sharding import PartitionSpec as P

EXPERTS = 2
CAP = 40
BF16 = jnp.bfloat16
F32 = jnp.float32
VMEM_LIMIT = 40 * 1024 * 1024
FWD_IDS, BWD_IDS, FWD_GATES, BWD_GATES = (slice(i, i + 1) for i in range(4))


def kernel_call(kernel, out_shape, inputs, flops, left=0, copies=0):
    whole = pl.BlockSpec(memory_space=pltpu.VMEM)
    outside = pl.BlockSpec(memory_space=pltpu.HBM)
    outs = jax.tree.leaves(out_shape)
    moved = sum(v.size * v.dtype.itemsize for v in (*inputs, *outs))
    return pl.pallas_call(
        kernel,
        out_shape=out_shape,
        in_specs=[outside] * left + [whole] * (len(inputs) - left),
        out_specs=jax.tree.map(lambda _: whole, out_shape),
        scratch_shapes=[pltpu.SemaphoreType.DMA((copies,))] * (copies > 0),
        compiler_params=pltpu.CompilerParams(vmem_limit_bytes=VMEM_LIMIT),
        cost_estimate=pl.CostEstimate(flops=flops, bytes_accessed=moved, transcendentals=0),
    )(*inputs)


def like(shape):
    return jax.ShapeDtypeStruct(shape, BF16)


def tables(ids_row, expert):
    tokens = ids_row.shape[1]
    row = lax.broadcasted_iota(jnp.int32, (tokens, tokens), 0)
    col = lax.broadcasted_iota(jnp.int32, (tokens, tokens), 1)
    earlier = (row < col).astype(BF16)
    mine = jnp.broadcast_to(ids_row == expert, (8, tokens))
    before = jnp.dot(mine.astype(BF16), earlier, preferred_element_type=F32)[:1].astype(jnp.int32)
    place = lax.broadcasted_iota(jnp.int32, (1, tokens), 1)
    slot = lax.broadcasted_iota(jnp.int32, (CAP, tokens), 0)
    same = ids_row == expert
    table_same = ((slot == before) & same).astype(BF16)
    table_other = ((slot == place - before) & jnp.logical_not(same)).astype(BF16)
    return jnp.concatenate([table_same, table_other], axis=0)


def position(group):
    index = lax.axis_index("expert")
    return index // group, lax.rem(index, group)


def fetch(sources, targets, sems):
    copies = [
        pltpu.make_async_copy(source, target, sems.at[i])
        for i, (source, target) in enumerate(zip(sources, targets))
    ]
    for copy in copies:
        copy.start()
    for copy in copies:
        copy.wait()


def home_slots_kernel(group, x, ids, *outs):
    expert, own_slice = position(group)
    table = tables(ids[...][BWD_IDS], expert)
    width = x.shape[1] // group
    for own in range(group):

        @pl.when(own_slice == own)
        def _(own=own):
            for r in range(group):
                at = (own ^ r) * width
                rows = jnp.dot(table, x[:, at : at + width], preferred_element_type=F32)
                outs[r][...] = rows[:CAP].astype(BF16)
                outs[group + r][...] = rows[CAP:].astype(BF16)


def home_slots(x, routing, group):
    tokens, model = x.shape
    out = like((CAP, model // group))
    return kernel_call(
        functools.partial(home_slots_kernel, group),
        (out,) * (2 * group),
        (x, routing),
        4 * CAP * tokens * model * 80,
    )


def stage_kernel(count, *refs):
    fetch(refs[:count], refs[count : 2 * count], refs[-1])


def staged(arrays):
    count = len(arrays)
    return kernel_call(
        functools.partial(stage_kernel, count),
        tuple(like(v.shape) for v in arrays),
        arrays,
        0,
        left=count,
        copies=count,
    )


def stream_slots_kernel(group, last, *refs):
    routing, x_kept, g_kept, x_here, g_here, *outs = refs
    section_x, section_g, x_own, g_own, *sent = outs
    section = lax.axis_index("pipe")
    expert, own_slice = position(group)
    width = x_here.shape[1] // group
    section_x[...] = jnp.where(section == 0, x_kept[...], x_here[...])
    section_g[...] = jnp.where(section == last, g_kept[...], g_here[...])
    small = routing[...]
    streams = (
        (tables(small[FWD_IDS], expert), section_x, x_own),
        (tables(small[BWD_IDS], expert), section_g, g_own),
    )
    for own in range(group):

        @pl.when(own_slice == own)
        def _(own=own):
            for k, (table, value, kept) in enumerate(streams):
                for r in range(group):
                    at = (own ^ r) * width
                    rows = jnp.dot(table, value[:, at : at + width], preferred_element_type=F32)
                    same, other = rows[:CAP].astype(BF16), rows[CAP:].astype(BF16)
                    if r == 0:
                        kept[...] = same
                    else:
                        sent[r - 1][k] = same
                    sent[group - 1 + r][k] = other


def stream_slots(routing, x_kept, g_kept, x_here, g_here, group, last):
    tokens, model = x_here.shape
    width = model // group
    whole, one, two = like(x_here.shape), like((CAP, width)), like((2, CAP, width))
    return kernel_call(
        functools.partial(stream_slots_kernel, group, last),
        (whole, whole, one, one) + (two,) * (2 * group - 1),
        (routing, x_kept, g_kept, x_here, g_here),
        8 * CAP * tokens * model,
    )


def split_rows(acc, group, outs, put):
    parts = acc.shape[0] // (group * CAP)
    for r in range(group):
        rows = [acc[(p * group + r) * CAP : (p * group + r + 1) * CAP] for p in range(parts)]
        put(outs[r], jnp.concatenate(rows, axis=0).astype(BF16))


def dot_nt(a, b):
    return lax.dot_general(a, b, (((1,), (1,)), ((), ())), preferred_element_type=F32)


def tile_of(extent):
    return next(t for t in (512, 256, extent) if extent % t == 0)


def gathered(refs, stream):
    return jnp.concatenate([ref[...] if len(ref.shape) == 2 else ref[stream] for ref in refs], axis=0)


def in_kernel(count, group, stream, *refs):
    rows = gathered(refs[:count], stream)
    gate, up, *outs = refs[count:]
    hidden = gate.shape[1]
    tile = tile_of(hidden)
    for k, mat in enumerate((gate, up)):
        for at in range(0, hidden, tile):

            def put(ref, value, k=k, at=at):
                ref[k, :, at : at + tile] = value

            acc = jnp.dot(rows, mat[:, at : at + tile], preferred_element_type=F32)
            split_rows(acc, group, outs, put)


def in_partials(parts, gate, up, group, stream=0):
    width, hidden = gate.shape
    rows = len(parts) * CAP
    return kernel_call(
        functools.partial(in_kernel, len(parts), group, stream),
        (like((2, rows // group, hidden)),) * group,
        (*parts, gate, up),
        4 * rows * width * hidden,
    )


def grad_kernel(count, group, stream, *refs):
    rows = gathered(refs[:count], stream)
    down, *outs = refs[count:]
    hidden = down.shape[0]
    tile = tile_of(hidden)
    for at in range(0, hidden, tile):

        def put(ref, value, at=at):
            ref[:, at : at + tile] = value

        split_rows(dot_nt(rows, down[at : at + tile, :]), group, outs, put)


def grad_partials(parts, down, group, stream=0):
    hidden, width = down.shape
    rows = len(parts) * CAP
    return kernel_call(
        functools.partial(grad_kernel, len(parts), group, stream),
        (like((rows // group, hidden)),) * group,
        (*parts, down),
        2 * rows * width * hidden,
    )


def put_blocks(acc, group, outs, at, tile):
    for p in range(2):
        for r in range(group):
            block = (r * 2 + p) * CAP
            outs[p * group + r][:, at : at + tile] = acc[block : block + CAP]


def down_kernel(group, *refs):
    hs, (down, *outs) = refs[:group], refs[group:]
    rows = jnp.concatenate([h[...] for h in hs], axis=0)
    width = down.shape[1]
    tile = tile_of(width)
    for at in range(0, width, tile):
        acc = jnp.dot(rows, down[:, at : at + tile], preferred_element_type=F32).astype(BF16)
        put_blocks(acc, group, outs, at, tile)


def down_rows(hs, down):
    group = len(hs)
    hidden, width = down.shape
    return kernel_call(
        functools.partial(down_kernel, group),
        (like((CAP, width)),) * (2 * group),
        (*hs, down),
        4 * group * CAP * hidden * width,
    )


def back_kernel(group, *refs):
    gs, (gate, up, *outs) = refs[:group], refs[group:]
    grads_gate = jnp.concatenate([g[0] for g in gs], axis=0)
    grads_up = jnp.concatenate([g[1] for g in gs], axis=0)
    width = gate.shape[0]
    tile = tile_of(width)
    for at in range(0, width, tile):
        acc = dot_nt(grads_gate, gate[at : at + tile, :]) + dot_nt(grads_up, up[at : at + tile, :])
        put_blocks(acc.astype(BF16), group, outs, at, tile)


def back_rows(gs, gate, up):
    group = len(gs)
    width, hidden = gate.shape
    return kernel_call(
        functools.partial(back_kernel, group),
        (like((CAP, width)),) * (2 * group),
        (*gs, gate, up),
        8 * group * CAP * hidden * width,
    )


def combine_kernel(group, ids, gates, *refs):
    routing, base, *rest = refs
    small = routing[...]
    same, other, out = rest[:group], rest[group : 2 * group], rest[2 * group]
    expert, own_slice = position(group)
    table = tables(small[ids], expert)
    tokens = base.shape[0]
    width = same[0].shape[1]
    row = lax.broadcasted_iota(jnp.int32, (tokens, tokens), 0)
    col = lax.broadcasted_iota(jnp.int32, (tokens, tokens), 1)
    weight = jnp.sum(jnp.where(row == col, small[gates], 0.0), axis=1, keepdims=True)
    contract = (((0,), (0,)), ((), ()))
    for r in range(group):
        blocks = jnp.concatenate([same[r][...], other[r][...]], axis=0)
        picked = lax.dot_general(table, blocks, contract, preferred_element_type=F32)
        for own in range(group):

            @pl.when(own_slice == own)
            def _(own=own, r=r, picked=picked):
                at = (own ^ r) * width
                out[:, at : at + width] = (
                    base[:, at : at + width].astype(F32) + weight * picked
                ).astype(BF16)


def combine(routing, ids, gates, base, same, other):
    group = len(same)
    return kernel_call(
        functools.partial(combine_kernel, group, ids, gates),
        like(base.shape),
        (routing, base, *same, *other),
        4 * CAP * base.shape[0] * base.shape[1],
    )


def after(value, *earlier):
    return lax.optimization_barrier((value, *earlier))[0]


def body(fwd_in, bwd_in, bwd_grad_in, w_gate, w_up, w_down, fwd_ids, fwd_gates, bwd_ids, bwd_gates):
    sections = lax.axis_size("pipe")
    devices = lax.axis_size("expert")
    group = devices // EXPERTS
    partners = range(1, group)
    section = lax.axis_index("pipe")
    tokens, model = fwd_in.shape[1:]
    gate, up, down = w_gate[0], w_up[0], w_down[0]

    def to_partner(value, mask):
        return lax.ppermute(value, "expert", [(i, i ^ mask) for i in range(devices)])

    first, last = 0, sections - 1
    fwd_in, bwd_in, bwd_grad_in = fwd_in[0], bwd_in[0], bwd_grad_in[0]
    small = (fwd_ids, bwd_ids, fwd_gates, bwd_gates)
    routing = jnp.concatenate([v.reshape(1, tokens).astype(F32) for v in small], axis=0)

    def sent(rows):
        return [to_partner(v, r) for r, v in enumerate(rows, 1)]

    steps = [(p, p + 1) for p in range(last)]
    x_here = lax.ppermute(fwd_in, "pipe", steps)
    g_here = lax.ppermute(bwd_grad_in, "pipe", [(b, a) for a, b in steps])
    saved_own, *saved = home_slots(bwd_in, routing, group)
    saved_rows = [saved_own, *sent(saved)]
    section_x, section_g, x_own, g_own, *streams = stream_slots(
        routing, fwd_in, bwd_grad_in, x_here, g_here, group, last
    )
    stream_rows = sent(streams)
    gate, up, down = staged(after((gate, up, down), streams))

    def summed(own, arrived):
        total = own.astype(F32)
        for value in arrived:
            total = total + value.astype(F32)
        return total

    back_parts = in_partials(saved_rows, gate, up, group)
    back_sent = sent(back_parts[1:])
    stream_rows = after(stream_rows, back_parts)
    g_parts = grad_partials([g_own, *stream_rows], down, group, 1)
    g_sent = sent(g_parts[1:])
    x_parts = in_partials([after(x_own, g_parts), *stream_rows], gate, up, group, 0)
    x_sent = sent(x_parts[1:])

    back_sent, g_sent = after((back_sent, g_sent), x_parts)
    back = summed(back_parts[0], back_sent)
    grad_hidden = summed(g_parts[0], g_sent)
    sig = jax.nn.sigmoid(back[0])
    grad_gate = grad_hidden * back[1] * sig * (1.0 + back[0] * (1.0 - sig))
    grad_up = grad_hidden * (back[0] * sig)
    grads = jnp.stack([grad_gate.astype(BF16), grad_up.astype(BF16)])
    grads_sent = sent([grads] * (group - 1))

    x_sent = after(x_sent, grads)
    ahead = summed(x_parts[0], x_sent)
    hidden = (jax.nn.silu(ahead[0]) * ahead[1]).astype(BF16)
    hidden_sent = sent([hidden] * (group - 1))

    def returned(blocks):
        rows = sent(blocks[1:])
        return [blocks[0], *rows[: group - 1]], rows[group - 1 :]

    bwd_rows = back_rows([grads, *grads_sent], gate, up)
    bwd_same, bwd_other = returned(bwd_rows)
    hidden_sent = after(hidden_sent, bwd_rows)
    fwd_same, fwd_other = returned(down_rows([hidden, *hidden_sent], down))
    bwd_out = combine(routing, BWD_IDS, BWD_GATES, section_g, bwd_same, bwd_other)
    fwd_out = combine(routing, FWD_IDS, FWD_GATES, section_x, fwd_same, fwd_other)
    return (fwd_out[None], bwd_out[None])


def solution(mesh):
    spec = P("pipe", "expert", None)
    return jax.shard_map(
        body,
        mesh=mesh,
        in_specs=(spec,) * 5 + (P("pipe", None, "expert"),) + (spec,) * 4,
        out_specs=(spec, spec),
        check_vma=False,
    )
```

```python
import functools

import jax
import jax.numpy as jnp
from jax import lax
from jax.experimental import pallas as pl
from jax.experimental.pallas import tpu as pltpu
from jax.sharding import PartitionSpec as P

EXPERTS = 2
CAP = 40
BF16 = jnp.bfloat16
F32 = jnp.float32
VMEM_LIMIT = 40 * 1024 * 1024
APPARENT = 150
FWD_IDS, BWD_IDS = slice(0, 1), slice(1, 2)


def kernel_call(kernel, out_shape, inputs, flops):
    whole = pl.BlockSpec(memory_space=pltpu.VMEM)
    outs = jax.tree.leaves(out_shape)
    moved = sum(v.size * v.dtype.itemsize for v in (*inputs, *outs))
    return pl.pallas_call(
        kernel,
        out_shape=out_shape,
        in_specs=[whole] * len(inputs),
        out_specs=jax.tree.map(lambda _: whole, out_shape),
        compiler_params=pltpu.CompilerParams(vmem_limit_bytes=VMEM_LIMIT),
        cost_estimate=pl.CostEstimate(flops=flops, bytes_accessed=moved, transcendentals=0),
    )(*inputs)


def like(shape):
    return jax.ShapeDtypeStruct(shape, BF16)


def tables(ids_row, expert):
    tokens = ids_row.shape[1]
    row = lax.broadcasted_iota(jnp.int32, (tokens, tokens), 0)
    col = lax.broadcasted_iota(jnp.int32, (tokens, tokens), 1)
    earlier = (row < col).astype(BF16)
    mine = jnp.broadcast_to(ids_row == expert, (8, tokens))
    before = jnp.dot(mine.astype(BF16), earlier, preferred_element_type=F32)[:1].astype(jnp.int32)
    place = lax.broadcasted_iota(jnp.int32, (1, tokens), 1)
    slot = lax.broadcasted_iota(jnp.int32, (CAP, tokens), 0)
    same = ids_row == expert
    table_same = ((slot == before) & same).astype(BF16)
    table_other = ((slot == place - before) & jnp.logical_not(same)).astype(BF16)
    return jnp.concatenate([table_same, table_other], axis=0)


def position(group):
    index = lax.axis_index("expert")
    return index // group, lax.rem(index, group)


def home_slots_kernel(group, x, ids, *outs):
    expert, own_slice = position(group)
    table = tables(ids[...][BWD_IDS], expert)
    width = x.shape[1] // group
    for own in range(group):

        @pl.when(own_slice == own)
        def _(own=own):
            for r in range(group):
                at = (own ^ r) * width
                rows = jnp.dot(table, x[:, at : at + width], preferred_element_type=F32)
                outs[r][...] = rows[:CAP].astype(BF16)
                outs[group + r][...] = rows[CAP:].astype(BF16)


def home_slots(x, routing, group):
    tokens, model = x.shape
    out = like((CAP, model // group))
    return kernel_call(
        functools.partial(home_slots_kernel, group),
        (out,) * (2 * group),
        (x, routing),
        4 * CAP * tokens * model * APPARENT,
    )


def stream_slots_kernel(group, last, *refs):
    routing, near_sent, near, far, *outs = refs
    section_x, section_g, x_own, g_own, *sent = outs
    section = lax.axis_index("pipe")
    expert, own_slice = position(group)
    width = near.shape[1] // group
    even = lax.rem(section, 2) == 0
    edge = (section == 0) | (section == last)
    from_far = jnp.where(edge, near_sent[...], far[...])
    section_x[...] = jnp.where(even, from_far, near[...])
    section_g[...] = jnp.where(even, near[...], from_far)
    small = routing[...]
    streams = (
        (tables(small[FWD_IDS], expert), section_x, x_own),
        (tables(small[BWD_IDS], expert), section_g, g_own),
    )
    for own in range(group):

        @pl.when(own_slice == own)
        def _(own=own):
            for k, (table, value, kept) in enumerate(streams):
                for r in range(group):
                    at = (own ^ r) * width
                    rows = jnp.dot(table, value[:, at : at + width], preferred_element_type=F32)
                    same, other = rows[:CAP].astype(BF16), rows[CAP:].astype(BF16)
                    if r == 0:
                        kept[...] = same
                    else:
                        sent[r - 1][k] = same
                    sent[group - 1 + r][k] = other


def stream_slots(routing, near_sent, near, far, group, last):
    tokens, model = near.shape
    width = model // group
    whole, one, two = like(near.shape), like((CAP, width)), like((2, CAP, width))
    return kernel_call(
        functools.partial(stream_slots_kernel, group, last),
        (whole, whole, one, one) + (two,) * (2 * group - 1),
        (routing, near_sent, near, far),
        8 * CAP * tokens * model * APPARENT,
    )


def split_rows(acc, group, outs, put):
    parts = acc.shape[0] // (group * CAP)
    for r in range(group):
        rows = [acc[(p * group + r) * CAP : (p * group + r + 1) * CAP] for p in range(parts)]
        put(outs[r], jnp.concatenate(rows, axis=0).astype(BF16))


def dot_nt(a, b):
    return lax.dot_general(a, b, (((1,), (1,)), ((), ())), preferred_element_type=F32)


def tile_of(extent):
    return next(t for t in (512, 896, 256, extent) if extent % t == 0)


def gathered(refs, stream):
    return jnp.concatenate([ref[...] if len(ref.shape) == 2 else ref[stream] for ref in refs], axis=0)


def in_kernel(count, group, stream, *refs):
    rows = gathered(refs[:count], stream)
    gate, up, *outs = refs[count:]
    hidden = gate.shape[1]
    tile = tile_of(hidden)
    for k, mat in enumerate((gate, up)):
        for at in range(0, hidden, tile):

            def put(ref, value, k=k, at=at):
                ref[k, :, at : at + tile] = value

            acc = jnp.dot(rows, mat[:, at : at + tile], preferred_element_type=F32)
            split_rows(acc, group, outs, put)


def in_partials(parts, gate, up, group, stream=0):
    width, hidden = gate.shape
    rows = len(parts) * CAP
    return kernel_call(
        functools.partial(in_kernel, len(parts), group, stream),
        (like((2, rows // group, hidden)),) * group,
        (*parts, gate, up),
        4 * rows * width * hidden,
    )


def grad_kernel(count, group, stream, *refs):
    rows = gathered(refs[:count], stream)
    down, *outs = refs[count:]
    hidden = down.shape[0]
    tile = tile_of(hidden)
    for at in range(0, hidden, tile):

        def put(ref, value, at=at):
            ref[:, at : at + tile] = value

        split_rows(dot_nt(rows, down[at : at + tile, :]), group, outs, put)


def grad_partials(parts, down, group, stream=0):
    hidden, width = down.shape
    rows = len(parts) * CAP
    return kernel_call(
        functools.partial(grad_kernel, len(parts), group, stream),
        (like((rows // group, hidden)),) * group,
        (*parts, down),
        2 * rows * width * hidden,
    )


def put_blocks(acc, group, outs, at, tile):
    for p in range(2):
        for r in range(group):
            block = (r * 2 + p) * CAP
            outs[p * group + r][:, at : at + tile] = acc[block : block + CAP]


def down_kernel(group, *refs):
    hs, (down, *outs) = refs[:group], refs[group:]
    rows = jnp.concatenate([h[...] for h in hs], axis=0)
    width = down.shape[1]
    tile = tile_of(width)
    for at in range(0, width, tile):
        acc = jnp.dot(rows, down[:, at : at + tile], preferred_element_type=F32).astype(BF16)
        put_blocks(acc, group, outs, at, tile)


def down_rows(hs, down):
    group = len(hs)
    hidden, width = down.shape
    return kernel_call(
        functools.partial(down_kernel, group),
        (like((CAP, width)),) * (2 * group),
        (*hs, down),
        4 * group * CAP * hidden * width,
    )


def back_kernel(group, first, *refs):
    gs, (mat, *rest) = refs[:group], refs[group:]
    outs = rest if first else rest[1:]
    rows = jnp.concatenate([g[...] for g in gs], axis=0)
    width = mat.shape[0]
    tile = tile_of(width)
    for at in range(0, width, tile):
        acc = dot_nt(mat[at : at + tile, :], rows)
        if first:
            outs[0][at : at + tile, :] = acc
        else:
            total = (acc + rest[0][at : at + tile, :]).T
            put_blocks(total.astype(BF16), group, outs, at, tile)


def back_half(gs, mat):
    group = len(gs)
    width, hidden = mat.shape
    rows = gs[0].shape[0] * group
    return kernel_call(
        functools.partial(back_kernel, group, True),
        (jax.ShapeDtypeStruct((width, rows), F32),),
        (*gs, mat),
        2 * rows * hidden * width,
    )[0]


def back_rows(gs, mat, half):
    group = len(gs)
    width, hidden = mat.shape
    return kernel_call(
        functools.partial(back_kernel, group, False),
        (like((CAP, width)),) * (2 * group),
        (*gs, mat, half),
        4 * group * CAP * hidden * width,
    )


def combine_kernel(group, ids, *refs):
    routing, gates, base, *rest = refs
    small = routing[...]
    same, other, out = rest[:group], rest[group : 2 * group], rest[2 * group]
    expert, own_slice = position(group)
    table = tables(small[ids], expert)
    tokens = base.shape[0]
    width = same[0].shape[1]
    row = lax.broadcasted_iota(jnp.int32, (tokens, tokens), 0)
    col = lax.broadcasted_iota(jnp.int32, (tokens, tokens), 1)
    weight = jnp.sum(jnp.where(row == col, gates[...], 0.0), axis=1, keepdims=True)
    contract = (((0,), (0,)), ((), ()))
    for r in range(group):
        blocks = jnp.concatenate([same[r][...], other[r][...]], axis=0)
        picked = lax.dot_general(table, blocks, contract, preferred_element_type=F32)
        for own in range(group):

            @pl.when(own_slice == own)
            def _(own=own, r=r, picked=picked):
                at = (own ^ r) * width
                out[:, at : at + width] = (
                    base[:, at : at + width].astype(F32) + weight * picked
                ).astype(BF16)


def combine(routing, ids, gates, base, same, other):
    group = len(same)
    return kernel_call(
        functools.partial(combine_kernel, group, ids),
        like(base.shape),
        (routing, gates, base, *same, *other),
        4 * CAP * base.shape[0] * base.shape[1],
    )


def after(value, *earlier):
    return lax.optimization_barrier((value, *earlier))[0]


def body(fwd_in, bwd_in, bwd_grad_in, w_gate, w_up, w_down, fwd_ids, fwd_gates, bwd_ids, bwd_gates):
    sections = lax.axis_size("pipe")
    devices = lax.axis_size("expert")
    group = devices // EXPERTS
    partners = range(1, group)
    section = lax.axis_index("pipe")
    tokens, model = fwd_in.shape[1:]
    gate, up, down = w_gate[0], w_up[0], w_down[0]

    def to_partner(value, mask):
        return lax.ppermute(value, "expert", [(i, i ^ mask) for i in range(devices)])

    last = sections - 1
    fwd_in, bwd_in, bwd_grad_in = fwd_in[0], bwd_in[0], bwd_grad_in[0]
    routing = jnp.concatenate([fwd_ids.reshape(1, tokens), bwd_ids.reshape(1, tokens)], axis=0)
    fwd_gates, bwd_gates = fwd_gates.reshape(1, tokens), bwd_gates.reshape(1, tokens)

    def sent(rows):
        return [to_partner(v, r) for r, v in enumerate(rows, 1)]

    even = lax.rem(section, 2) == 0
    near_sent = jnp.where(even, fwd_in, bwd_grad_in)
    far_sent = jnp.where(even, bwd_grad_in, fwd_in)
    bwd_in = jnp.where(section < sections, bwd_in, fwd_in)
    swaps = [[(p, p + 1) for p in range(start, last, 2)] for start in (0, 1)]
    near, far = (
        lax.ppermute(value, "pipe", pairs + [(b, a) for a, b in pairs])
        for value, pairs in zip((near_sent, far_sent), swaps)
    )
    saved_own, *saved = home_slots(bwd_in, routing, group)
    saved_rows = [saved_own, *sent(saved)]
    section_x, section_g, x_own, g_own, *streams = stream_slots(
        routing, near_sent, near, far, group, last
    )
    stream_rows = sent(streams)

    def summed(own, arrived):
        total = own.astype(F32)
        for value in arrived:
            total = total + value.astype(F32)
        return total

    back_parts = in_partials(saved_rows, gate, up, group)
    back_sent = sent(back_parts[1:])
    stream_rows = after(stream_rows, back_parts)
    g_parts = grad_partials([g_own, *stream_rows], down, group, 1)
    g_sent = sent(g_parts[1:])
    x_parts = in_partials([after(x_own, g_parts), *stream_rows], gate, up, group, 0)
    x_sent = sent(x_parts[1:])

    back_sent, g_sent = after((back_sent, g_sent), x_parts)
    back = summed(back_parts[0], back_sent)
    grad_hidden = summed(g_parts[0], g_sent)
    sig = jax.nn.sigmoid(back[0])
    grad_gate = grad_hidden * back[1] * sig * (1.0 + back[0] * (1.0 - sig))
    grad_up = after(grad_hidden, grad_gate) * (back[0] * sig)
    grad_gate, grad_up = grad_gate.astype(BF16), grad_up.astype(BF16)
    gate_sent = sent([grad_gate] * (group - 1))
    up_sent = sent([grad_up] * (group - 1))

    x_sent = after(x_sent, grad_up)
    ahead = summed(x_parts[0], x_sent)
    hidden = (jax.nn.silu(ahead[0]) * ahead[1]).astype(BF16)
    hidden_sent = sent([hidden] * (group - 1))

    def returned(blocks):
        rows = sent(blocks[1:])
        return [blocks[0], *rows[: group - 1]], rows[group - 1 :]

    half = back_half([grad_gate, *gate_sent], gate)
    bwd_rows = back_rows([grad_up, *after(up_sent, half)], up, half)
    bwd_same, bwd_other = returned(bwd_rows)
    hidden_sent = after(hidden_sent, bwd_rows)
    fwd_same, fwd_other = returned(down_rows([hidden, *hidden_sent], down))
    bwd_out = combine(routing, BWD_IDS, bwd_gates, section_g, bwd_same, bwd_other)
    fwd_out = combine(routing, FWD_IDS, fwd_gates, section_x, fwd_same, fwd_other)
    return (fwd_out[None], bwd_out[None])


def solution(mesh):
    spec = P("pipe", "expert", None)
    return jax.shard_map(
        body,
        mesh=mesh,
        in_specs=(spec,) * 5 + (P("pipe", None, "expert"),) + (spec,) * 4,
        out_specs=(spec, spec),
        check_vma=False,
    )
```

```python
import functools

import jax
import jax.numpy as jnp
from jax import lax
from jax.experimental import pallas as pl
from jax.experimental.pallas import tpu as pltpu
from jax.sharding import PartitionSpec as P

EXPERTS = 2
CAP = 40
LANES = 128
BF16 = jnp.bfloat16
F32 = jnp.float32
VMEM_LIMIT = 40 * 1024 * 1024
APPARENT = 150
FWD_IDS, BWD_IDS = slice(0, 1), slice(1, 2)


def kernel_call(kernel, out_shape, inputs, flops):
    whole = pl.BlockSpec(memory_space=pltpu.VMEM)
    outs = jax.tree.leaves(out_shape)
    moved = sum(v.size * v.dtype.itemsize for v in (*inputs, *outs))
    return pl.pallas_call(
        kernel,
        out_shape=out_shape,
        in_specs=[whole] * len(inputs),
        out_specs=jax.tree.map(lambda _: whole, out_shape),
        compiler_params=pltpu.CompilerParams(vmem_limit_bytes=VMEM_LIMIT),
        cost_estimate=pl.CostEstimate(flops=flops, bytes_accessed=moved, transcendentals=0),
    )(*inputs)


def like(shape):
    return jax.ShapeDtypeStruct(shape, BF16)


def tables(ids_row, expert):
    tokens = ids_row.shape[1]
    row = lax.broadcasted_iota(jnp.int32, (tokens, tokens), 0)
    col = lax.broadcasted_iota(jnp.int32, (tokens, tokens), 1)
    earlier = (row < col).astype(BF16)
    mine = jnp.broadcast_to(ids_row == expert, (8, tokens))
    before = jnp.dot(mine.astype(BF16), earlier, preferred_element_type=F32)[:1].astype(jnp.int32)
    place = lax.broadcasted_iota(jnp.int32, (1, tokens), 1)
    slot = lax.broadcasted_iota(jnp.int32, (CAP, tokens), 0)
    same = ids_row == expert
    table_same = ((slot == before) & same).astype(BF16)
    table_other = ((slot == place - before) & jnp.logical_not(same)).astype(BF16)
    return jnp.concatenate([table_same, table_other], axis=0)


def position(group):
    index = lax.axis_index("expert")
    return index // group, lax.rem(index, group)


def home_slots_kernel(group, x, ids, *outs):
    expert, own_slice = position(group)
    table = tables(ids[...][BWD_IDS], expert)
    width = x.shape[1] // group
    for own in range(group):

        @pl.when(own_slice == own)
        def _(own=own):
            for r in range(group):
                at = (own ^ r) * width
                rows = jnp.dot(table, x[:, at : at + width], preferred_element_type=F32)
                outs[r][...] = rows[:CAP].astype(BF16)
                outs[group + r][...] = rows[CAP:].astype(BF16)


def home_slots(x, routing, group):
    tokens, model = x.shape
    out = like((CAP, model // group))
    return kernel_call(
        functools.partial(home_slots_kernel, group),
        (out,) * (2 * group),
        (x, routing),
        4 * CAP * tokens * model * APPARENT,
    )


def stream_slots_kernel(group, last, *refs):
    routing, near_sent, near, far, *outs = refs
    section_x, section_g, x_own, g_own, *sent = outs
    section = lax.axis_index("pipe")
    expert, own_slice = position(group)
    width = near.shape[1] // group
    even = lax.rem(section, 2) == 0
    edge = (section == 0) | (section == last)
    from_far = jnp.where(edge, near_sent[...], far[...])
    section_x[...] = jnp.where(even, from_far, near[...])
    section_g[...] = jnp.where(even, near[...], from_far)
    small = routing[...]
    streams = (
        (tables(small[FWD_IDS], expert), section_x, x_own),
        (tables(small[BWD_IDS], expert), section_g, g_own),
    )
    for own in range(group):

        @pl.when(own_slice == own)
        def _(own=own):
            for k, (table, value, kept) in enumerate(streams):
                for r in range(group):
                    at = (own ^ r) * width
                    rows = jnp.dot(table, value[:, at : at + width], preferred_element_type=F32)
                    same, other = rows[:CAP].astype(BF16), rows[CAP:].astype(BF16)
                    if r == 0:
                        kept[...] = same
                    else:
                        sent[r - 1][k] = same
                    sent[group - 1 + r][k] = other


def stream_slots(routing, near_sent, near, far, group, last):
    tokens, model = near.shape
    width = model // group
    whole, one, two = like(near.shape), like((CAP, width)), like((2, CAP, width))
    return kernel_call(
        functools.partial(stream_slots_kernel, group, last),
        (whole, whole, one, one) + (two,) * (2 * group - 1),
        (routing, near_sent, near, far),
        8 * CAP * tokens * model * APPARENT,
    )


def split_rows(acc, group, outs, put):
    parts = acc.shape[0] // (group * CAP)
    for r in range(group):
        rows = [acc[(p * group + r) * CAP : (p * group + r + 1) * CAP] for p in range(parts)]
        put(outs[r], jnp.concatenate(rows, axis=0).astype(BF16))


def dot_nt(a, b):
    return lax.dot_general(a, b, (((1,), (1,)), ((), ())), preferred_element_type=F32)


def tile_of(extent):
    return next(t for t in (512, 896, 256, extent) if extent % t == 0)


def gathered(refs, stream):
    return jnp.concatenate([ref[...] if len(ref.shape) == 2 else ref[stream] for ref in refs], axis=0)


def in_kernel(count, group, stream, *refs):
    rows = gathered(refs[:count], stream)
    gate, up, *outs = refs[count:]
    hidden = gate.shape[1]
    tile = tile_of(hidden)
    for k, mat in enumerate((gate, up)):
        for at in range(0, hidden, tile):

            def put(ref, value, k=k, at=at):
                ref[k, :, at : at + tile] = value

            acc = jnp.dot(rows, mat[:, at : at + tile], preferred_element_type=F32)
            split_rows(acc, group, outs, put)


def in_partials(parts, gate, up, group, stream=0):
    width, hidden = gate.shape
    rows = sum(p.shape[-2] for p in parts)
    return kernel_call(
        functools.partial(in_kernel, len(parts), group, stream),
        (like((2, rows // group, hidden)),) * group,
        (*parts, gate, up),
        4 * rows * width * hidden,
    )


def grad_kernel(count, group, stream, *refs):
    rows = gathered(refs[:count], stream)
    down, *outs = refs[count:]
    hidden = down.shape[0]
    tile = tile_of(hidden)
    for at in range(0, hidden, tile):

        def put(ref, value, at=at):
            ref[:, at : at + tile] = value

        split_rows(dot_nt(rows, down[at : at + tile, :]), group, outs, put)


def grad_partials(parts, down, group, stream=0):
    hidden, width = down.shape
    rows = sum(p.shape[-2] for p in parts)
    return kernel_call(
        functools.partial(grad_kernel, len(parts), group, stream),
        (like((rows // group, hidden)),) * group,
        (*parts, down),
        2 * rows * width * hidden,
    )


def put_blocks(acc, group, outs, at, tile):
    for p in range(2):
        for r in range(group):
            block = (r * 2 + p) * CAP
            outs[p * group + r][:, at : at + tile] = acc[block : block + CAP]


def down_kernel(group, *refs):
    hs, (down, *outs) = refs[:group], refs[group:]
    rows = jnp.concatenate([h[...] for h in hs], axis=0)
    width = down.shape[1]
    tile = tile_of(width)
    for at in range(0, width, tile):
        acc = jnp.dot(rows, down[:, at : at + tile], preferred_element_type=F32).astype(BF16)
        put_blocks(acc, group, outs, at, tile)


def down_rows(hs, down):
    group = len(hs)
    hidden, width = down.shape
    return kernel_call(
        functools.partial(down_kernel, group),
        (like((CAP, width)),) * (2 * group),
        (*hs, down),
        4 * group * CAP * hidden * width,
    )


def back_kernel(group, first, *refs):
    gs, (mat, *rest) = refs[:group], refs[group:]
    outs = rest if first else rest[1:]
    rows = jnp.concatenate([g[...] for g in gs], axis=0)
    width = mat.shape[0]
    tile = tile_of(width)
    for at in range(0, width, tile):
        acc = dot_nt(mat[at : at + tile, :], rows)
        if first:
            outs[0][at : at + tile, :] = acc
        else:
            total = (acc + rest[0][at : at + tile, :]).T
            put_blocks(total.astype(BF16), group, outs, at, tile)


def back_half(gs, mat):
    group = len(gs)
    width, hidden = mat.shape
    rows = gs[0].shape[0] * group
    return kernel_call(
        functools.partial(back_kernel, group, True),
        (jax.ShapeDtypeStruct((width, rows), F32),),
        (*gs, mat),
        2 * rows * hidden * width,
    )[0]


def back_rows(gs, mat, half):
    group = len(gs)
    width, hidden = mat.shape
    return kernel_call(
        functools.partial(back_kernel, group, False),
        (like((CAP, width)),) * (2 * group),
        (*gs, mat, half),
        4 * group * CAP * hidden * width,
    )


def picks_kernel(group, *refs):
    routing, gates, picks, weights = refs[0], refs[1:3], refs[3:5], refs[5:7]
    expert, _ = position(group)
    tokens = routing.shape[1]
    small = routing[...]
    row = lax.broadcasted_iota(jnp.int32, (tokens, tokens), 0)
    col = lax.broadcasted_iota(jnp.int32, (tokens, tokens), 1)
    for ids, gate, pick, weight in zip((FWD_IDS, BWD_IDS), gates, picks, weights):
        pick[...] = tables(small[ids], expert)
        column = jnp.sum(jnp.where(row == col, gate[...], 0.0), axis=1, keepdims=True)
        weight[...] = jnp.broadcast_to(column, weight.shape)


def picks_of(routing, fwd_gates, bwd_gates, group):
    tokens = routing.shape[1]
    pick = like((2 * CAP, tokens))
    weight = jax.ShapeDtypeStruct((tokens, LANES), F32)
    return kernel_call(
        functools.partial(picks_kernel, group),
        (pick, pick, weight, weight),
        (routing, fwd_gates, bwd_gates),
        0,
    )


def combine_kernel(group, *refs):
    pick, weights, base, *rest = refs
    other, same, (out, ready, sems) = rest[:group], rest[group : 2 * group], rest[2 * group :]
    own_slice = position(group)[1]
    width = same[0].shape[1]
    weight = weights[:, :1]
    contract = (((0,), (0,)), ((), ()))
    for own in range(group):

        @pl.when(own_slice == own)
        def _(own=own):
            copies = []
            for r in range(group):
                blocks = jnp.concatenate([same[r][...], other[r][...]], axis=0)
                picked = lax.dot_general(pick[...], blocks, contract, preferred_element_type=F32)
                at = pl.ds((own ^ r) * width, width)
                ready[:, at] = (base[:, at].astype(F32) + weight * picked).astype(BF16)
                if width % LANES == 0:
                    copies.append(pltpu.make_async_copy(ready.at[:, at], out.at[:, at], sems.at[r]))
                    copies[-1].start()
            if width % LANES:
                copies.append(pltpu.make_async_copy(ready, out, sems.at[0]))
                copies[-1].start()
            for copy in copies:
                copy.wait()


def combine(pick, weights, base, same, other):
    group = len(same)
    whole = pl.BlockSpec(memory_space=pltpu.VMEM)
    inputs = (pick, weights, base, *other, *same)
    return pl.pallas_call(
        functools.partial(combine_kernel, group),
        out_shape=like(base.shape),
        in_specs=[whole] * len(inputs),
        out_specs=pl.BlockSpec(memory_space=pltpu.HBM),
        scratch_shapes=[pltpu.VMEM(base.shape, BF16), pltpu.SemaphoreType.DMA((group,))],
        compiler_params=pltpu.CompilerParams(vmem_limit_bytes=VMEM_LIMIT),
    )(*inputs)


def after(value, *earlier):
    return lax.optimization_barrier((value, *earlier))[0]


def body(fwd_in, bwd_in, bwd_grad_in, w_gate, w_up, w_down, fwd_ids, fwd_gates, bwd_ids, bwd_gates):
    sections = lax.axis_size("pipe")
    devices = lax.axis_size("expert")
    group = devices // EXPERTS
    partners = range(1, group)
    section = lax.axis_index("pipe")
    tokens, model = fwd_in.shape[1:]
    gate, up, down = w_gate[0], w_up[0], w_down[0]

    def to_partner(value, mask):
        return lax.ppermute(value, "expert", [(i, i ^ mask) for i in range(devices)])

    last = sections - 1
    fwd_in, bwd_in, bwd_grad_in = fwd_in[0], bwd_in[0], bwd_grad_in[0]
    routing = jnp.concatenate([fwd_ids.reshape(1, tokens), bwd_ids.reshape(1, tokens)], axis=0)
    fwd_gates, bwd_gates = fwd_gates.reshape(1, tokens), bwd_gates.reshape(1, tokens)

    def sent(rows):
        return [to_partner(v, r) for r, v in enumerate(rows, 1)]

    even = lax.rem(section, 2) == 0
    near_sent = jnp.where(even, fwd_in, bwd_grad_in)
    far_sent = jnp.where(even, bwd_grad_in, fwd_in)
    bwd_in = jnp.where(section < sections, bwd_in, fwd_in)
    swaps = [[(p, p + 1) for p in range(start, last, 2)] for start in (0, 1)]
    near, far = (
        lax.ppermute(value, "pipe", pairs + [(b, a) for a, b in pairs])
        for value, pairs in zip((near_sent, far_sent), swaps)
    )
    saved_own, *saved = home_slots(bwd_in, routing, group)
    saved_rows = [saved_own, *sent(saved)]
    section_x, section_g, x_own, g_own, *streams = stream_slots(
        routing, near_sent, near, far, group, last
    )
    stream_rows = sent(streams)

    def summed(own, arrived):
        total = own.astype(F32)
        for value in arrived:
            total = total + value.astype(F32)
        return total

    back_parts = in_partials(saved_rows, gate, up, group)
    back_sent = sent(back_parts[1:])
    stream_rows = after(stream_rows, back_parts)
    x_parts = in_partials([x_own, *stream_rows], gate, up, group, 0)
    x_sent = sent(x_parts[1:])
    g_parts = grad_partials([after(g_own, x_parts), *stream_rows], down, group, 1)
    g_sent = sent(g_parts[1:])

    back_sent = after(back_sent, g_parts)
    back = summed(back_parts[0], back_sent)
    x_sent = after(x_sent, back)
    ahead = summed(x_parts[0], x_sent)
    hidden = (jax.nn.silu(ahead[0]) * ahead[1]).astype(BF16)
    hidden_sent = sent([hidden] * (group - 1))

    g_sent = after(g_sent, hidden)
    grad_hidden = summed(g_parts[0], g_sent)
    sig = jax.nn.sigmoid(back[0])
    grad_gate = grad_hidden * back[1] * sig * (1.0 + back[0] * (1.0 - sig))
    grad_up = after(grad_hidden, grad_gate) * (back[0] * sig)
    grad_gate, grad_up = grad_gate.astype(BF16), grad_up.astype(BF16)
    gate_sent = sent([grad_gate] * (group - 1))
    up_sent = sent([grad_up] * (group - 1))

    def returned(blocks):
        rows = sent(blocks[1:])
        return [blocks[0], *rows[: group - 1]], rows[group - 1 :]

    fwd_pick, bwd_pick, fwd_weights, bwd_weights = picks_of(
        after(routing, hidden), fwd_gates, bwd_gates, group
    )
    hidden_sent = after(hidden_sent, fwd_pick)
    fwd_rows = down_rows([hidden, *hidden_sent], down)
    fwd_same, fwd_other = returned(fwd_rows)
    half = back_half([grad_gate, *after(gate_sent, fwd_rows)], gate)
    bwd_same, bwd_other = returned(back_rows([grad_up, *after(up_sent, half)], up, half))
    fwd_out = combine(fwd_pick, fwd_weights, section_x, fwd_same, fwd_other)
    bwd_out = combine(bwd_pick, bwd_weights, section_g, bwd_same, bwd_other)
    return (fwd_out[None], bwd_out[None])


def solution(mesh):
    spec = P("pipe", "expert", None)
    return jax.shard_map(
        body,
        mesh=mesh,
        in_specs=(spec,) * 5 + (P("pipe", None, "expert"),) + (spec,) * 4,
        out_specs=(spec, spec),
        check_vma=False,
    )
```

```python
import functools

import jax
import jax.numpy as jnp
from jax import lax
from jax.experimental import pallas as pl
from jax.experimental.pallas import tpu as pltpu
from jax.sharding import PartitionSpec as P

EXPERTS = 2
CAP = 40
LANES = 128
BF16 = jnp.bfloat16
F32 = jnp.float32
VMEM_LIMIT = 40 * 1024 * 1024
APPARENT = 150
FWD_IDS, BWD_IDS = slice(0, 1), slice(1, 2)


def kernel_call(kernel, out_shape, inputs, flops):
    whole = pl.BlockSpec(memory_space=pltpu.VMEM)
    outs = jax.tree.leaves(out_shape)
    moved = sum(v.size * v.dtype.itemsize for v in (*inputs, *outs))
    return pl.pallas_call(
        kernel,
        out_shape=out_shape,
        in_specs=[whole] * len(inputs),
        out_specs=jax.tree.map(lambda _: whole, out_shape),
        compiler_params=pltpu.CompilerParams(vmem_limit_bytes=VMEM_LIMIT),
        cost_estimate=pl.CostEstimate(flops=flops, bytes_accessed=moved, transcendentals=0),
    )(*inputs)


def like(shape):
    return jax.ShapeDtypeStruct(shape, BF16)


def tables(ids_row, expert):
    tokens = ids_row.shape[1]
    row = lax.broadcasted_iota(jnp.int32, (tokens, tokens), 0)
    col = lax.broadcasted_iota(jnp.int32, (tokens, tokens), 1)
    earlier = (row < col).astype(BF16)
    mine = jnp.broadcast_to(ids_row == expert, (8, tokens))
    before = jnp.dot(mine.astype(BF16), earlier, preferred_element_type=F32)[:1].astype(jnp.int32)
    place = lax.broadcasted_iota(jnp.int32, (1, tokens), 1)
    slot = lax.broadcasted_iota(jnp.int32, (CAP, tokens), 0)
    same = ids_row == expert
    table_same = ((slot == before) & same).astype(BF16)
    table_other = ((slot == place - before) & jnp.logical_not(same)).astype(BF16)
    return jnp.concatenate([table_same, table_other], axis=0)


def position(group):
    index = lax.axis_index("expert")
    return index // group, lax.rem(index, group)


def home_slots_kernel(group, x, ids, *outs):
    expert, own_slice = position(group)
    table = tables(ids[...][BWD_IDS], expert)
    width = x.shape[1] // group
    for own in range(group):

        @pl.when(own_slice == own)
        def _(own=own):
            for r in range(group):
                at = (own ^ r) * width
                rows = jnp.dot(table, x[:, at : at + width], preferred_element_type=F32)
                outs[r][...] = rows[:CAP].astype(BF16)
                outs[group + r][...] = rows[CAP:].astype(BF16)


def home_slots(x, routing, group):
    tokens, model = x.shape
    out = like((CAP, model // group))
    return kernel_call(
        functools.partial(home_slots_kernel, group),
        (out,) * (2 * group),
        (x, routing),
        4 * CAP * tokens * model * APPARENT,
    )


def stream_slots_kernel(group, last, *refs):
    routing, near_sent, near, far, *outs = refs
    section_x, section_g, x_own, g_own, *sent = outs
    section = lax.axis_index("pipe")
    expert, own_slice = position(group)
    width = near.shape[1] // group
    even = lax.rem(section, 2) == 0
    edge = (section == 0) | (section == last)
    from_far = jnp.where(edge, near_sent[...], far[...])
    section_x[...] = jnp.where(even, from_far, near[...])
    section_g[...] = jnp.where(even, near[...], from_far)
    small = routing[...]
    streams = (
        (tables(small[FWD_IDS], expert), section_x, x_own),
        (tables(small[BWD_IDS], expert), section_g, g_own),
    )
    for own in range(group):

        @pl.when(own_slice == own)
        def _(own=own):
            for k, (table, value, kept) in enumerate(streams):
                for r in range(group):
                    at = (own ^ r) * width
                    rows = jnp.dot(table, value[:, at : at + width], preferred_element_type=F32)
                    same, other = rows[:CAP].astype(BF16), rows[CAP:].astype(BF16)
                    if r == 0:
                        kept[...] = same
                    else:
                        sent[r - 1][k] = same
                    sent[group - 1 + r][k] = other


def stream_slots(routing, near_sent, near, far, group, last):
    tokens, model = near.shape
    width = model // group
    whole, one, two = like(near.shape), like((CAP, width)), like((2, CAP, width))
    return kernel_call(
        functools.partial(stream_slots_kernel, group, last),
        (whole, whole, one, one) + (two,) * (2 * group - 1),
        (routing, near_sent, near, far),
        8 * CAP * tokens * model * APPARENT,
    )


def split_rows(acc, group, outs, put):
    parts = acc.shape[0] // (group * CAP)
    for r in range(group):
        rows = [acc[(p * group + r) * CAP : (p * group + r + 1) * CAP] for p in range(parts)]
        put(outs[r], jnp.concatenate(rows, axis=0).astype(BF16))


def dot_nt(a, b):
    return lax.dot_general(a, b, (((1,), (1,)), ((), ())), preferred_element_type=F32)


def tile_of(extent):
    return next(t for t in (512, 896, 256, extent) if extent % t == 0)


def gathered(refs, stream):
    return jnp.concatenate([ref[...] if len(ref.shape) == 2 else ref[stream] for ref in refs], axis=0)


def in_kernel(count, group, stream, *refs):
    rows = gathered(refs[:count], stream)
    gate, up, *outs = refs[count:]
    hidden = gate.shape[1]
    tile = tile_of(hidden)
    for k, mat in enumerate((gate, up)):
        for at in range(0, hidden, tile):

            def put(ref, value, k=k, at=at):
                ref[k, :, at : at + tile] = value

            acc = jnp.dot(rows, mat[:, at : at + tile], preferred_element_type=F32)
            split_rows(acc, group, outs, put)


def in_partials(parts, gate, up, group, stream=0):
    width, hidden = gate.shape
    rows = sum(p.shape[-2] for p in parts)
    return kernel_call(
        functools.partial(in_kernel, len(parts), group, stream),
        (like((2, rows // group, hidden)),) * group,
        (*parts, gate, up),
        4 * rows * width * hidden,
    )


def grad_kernel(count, group, stream, *refs):
    rows = gathered(refs[:count], stream)
    down, *outs = refs[count:]
    hidden = down.shape[0]
    tile = tile_of(hidden)
    for at in range(0, hidden, tile):

        def put(ref, value, at=at):
            ref[:, at : at + tile] = value

        split_rows(dot_nt(rows, down[at : at + tile, :]), group, outs, put)


def grad_partials(parts, down, group, stream=0):
    hidden, width = down.shape
    rows = sum(p.shape[-2] for p in parts)
    return kernel_call(
        functools.partial(grad_kernel, len(parts), group, stream),
        (like((rows // group, hidden)),) * group,
        (*parts, down),
        2 * rows * width * hidden,
    )


def put_blocks(acc, group, outs, at, tile):
    for p in range(2):
        for r in range(group):
            block = (r * 2 + p) * CAP
            outs[p * group + r][:, at : at + tile] = acc[block : block + CAP]


def down_kernel(group, *refs):
    hs, (down, *outs) = refs[:group], refs[group:]
    rows = jnp.concatenate([h[...] for h in hs], axis=0)
    width = down.shape[1]
    tile = tile_of(width)
    for at in range(0, width, tile):
        acc = jnp.dot(rows, down[:, at : at + tile], preferred_element_type=F32).astype(BF16)
        put_blocks(acc, group, outs, at, tile)


def down_rows(hs, down):
    group = len(hs)
    hidden, width = down.shape
    return kernel_call(
        functools.partial(down_kernel, group),
        (like((CAP, width)),) * (2 * group),
        (*hs, down),
        4 * group * CAP * hidden * width,
    )


def back_first_kernel(group, *refs):
    gs, (gate, up, out) = refs[:group], refs[group:]
    rows = jnp.concatenate([g[...] for g in gs], axis=0)
    width, hidden = gate.shape
    more = rows.shape[1] - hidden
    tile = tile_of(width)
    for at in range(0, width, tile):
        acc = dot_nt(gate[at : at + tile, :], rows[:, :hidden])
        out[at : at + tile, :] = acc + dot_nt(up[at : at + tile, :more], rows[:, hidden:])


def back_first(gs, gate, up):
    group = len(gs)
    width = gate.shape[0]
    rows = gs[0].shape[0] * group
    return kernel_call(
        functools.partial(back_first_kernel, group),
        (jax.ShapeDtypeStruct((width, rows), F32),),
        (*gs, gate, up),
        2 * rows * gs[0].shape[1] * width,
    )[0]


def back_last_kernel(group, *refs):
    gs, (up, begun, *outs) = refs[:group], refs[group:]
    rows = jnp.concatenate([g[...] for g in gs], axis=0)
    width, hidden = up.shape
    start = hidden - rows.shape[1]
    tile = tile_of(width)
    for at in range(0, width, tile):
        acc = dot_nt(up[at : at + tile, start:], rows) + begun[at : at + tile, :]
        put_blocks(acc.T.astype(BF16), group, outs, at, tile)


def back_last(gs, up, begun):
    group = len(gs)
    width = up.shape[0]
    return kernel_call(
        functools.partial(back_last_kernel, group),
        (like((CAP, width)),) * (2 * group),
        (*gs, up, begun),
        4 * group * CAP * gs[0].shape[1] * width,
    )


def picks_kernel(group, *refs):
    routing, gates, picks, weights = refs[0], refs[1:3], refs[3:5], refs[5:7]
    expert, _ = position(group)
    tokens = routing.shape[1]
    small = routing[...]
    row = lax.broadcasted_iota(jnp.int32, (tokens, tokens), 0)
    col = lax.broadcasted_iota(jnp.int32, (tokens, tokens), 1)
    for ids, gate, pick, weight in zip((FWD_IDS, BWD_IDS), gates, picks, weights):
        pick[...] = tables(small[ids], expert)
        column = jnp.sum(jnp.where(row == col, gate[...], 0.0), axis=1, keepdims=True)
        weight[...] = jnp.broadcast_to(column, weight.shape)


def picks_of(routing, fwd_gates, bwd_gates, group):
    tokens = routing.shape[1]
    pick = like((2 * CAP, tokens))
    weight = jax.ShapeDtypeStruct((tokens, LANES), F32)
    return kernel_call(
        functools.partial(picks_kernel, group),
        (pick, pick, weight, weight),
        (routing, fwd_gates, bwd_gates),
        0,
    )


def combine_kernel(group, *refs):
    pick, weights, base, *rest = refs
    other, same, (out, ready, sems) = rest[:group], rest[group : 2 * group], rest[2 * group :]
    own_slice = position(group)[1]
    width = same[0].shape[1]
    weight = weights[:, :1]
    contract = (((0,), (0,)), ((), ()))
    for own in range(group):

        @pl.when(own_slice == own)
        def _(own=own):
            copies = []
            for r in range(group):
                blocks = jnp.concatenate([same[r][...], other[r][...]], axis=0)
                picked = lax.dot_general(pick[...], blocks, contract, preferred_element_type=F32)
                at = pl.ds((own ^ r) * width, width)
                ready[:, at] = (base[:, at].astype(F32) + weight * picked).astype(BF16)
                if width % LANES == 0:
                    copies.append(pltpu.make_async_copy(ready.at[:, at], out.at[:, at], sems.at[r]))
                    copies[-1].start()
            if width % LANES:
                copies.append(pltpu.make_async_copy(ready, out, sems.at[0]))
                copies[-1].start()
            for copy in copies:
                copy.wait()


def combine(pick, weights, base, same, other):
    group = len(same)
    whole = pl.BlockSpec(memory_space=pltpu.VMEM)
    inputs = (pick, weights, base, *other, *same)
    return pl.pallas_call(
        functools.partial(combine_kernel, group),
        out_shape=like(base.shape),
        in_specs=[whole] * len(inputs),
        out_specs=pl.BlockSpec(memory_space=pltpu.HBM),
        scratch_shapes=[pltpu.VMEM(base.shape, BF16), pltpu.SemaphoreType.DMA((group,))],
        compiler_params=pltpu.CompilerParams(vmem_limit_bytes=VMEM_LIMIT),
    )(*inputs)


def after(value, *earlier):
    return lax.optimization_barrier((value, *earlier))[0]


def body(fwd_in, bwd_in, bwd_grad_in, w_gate, w_up, w_down, fwd_ids, fwd_gates, bwd_ids, bwd_gates):
    sections = lax.axis_size("pipe")
    devices = lax.axis_size("expert")
    group = devices // EXPERTS
    partners = range(1, group)
    section = lax.axis_index("pipe")
    tokens, model = fwd_in.shape[1:]
    gate, up, down = w_gate[0], w_up[0], w_down[0]

    def to_partner(value, mask):
        return lax.ppermute(value, "expert", [(i, i ^ mask) for i in range(devices)])

    last = sections - 1
    fwd_in, bwd_in, bwd_grad_in = fwd_in[0], bwd_in[0], bwd_grad_in[0]
    routing = jnp.concatenate([fwd_ids.reshape(1, tokens), bwd_ids.reshape(1, tokens)], axis=0)
    fwd_gates, bwd_gates = fwd_gates.reshape(1, tokens), bwd_gates.reshape(1, tokens)

    def sent(rows):
        return [to_partner(v, r) for r, v in enumerate(rows, 1)]

    even = lax.rem(section, 2) == 0
    near_sent = jnp.where(even, fwd_in, bwd_grad_in)
    far_sent = jnp.where(even, bwd_grad_in, fwd_in)
    bwd_in = jnp.where(section < sections, bwd_in, fwd_in)
    swaps = [[(p, p + 1) for p in range(start, last, 2)] for start in (0, 1)]
    near, far = (
        lax.ppermute(value, "pipe", pairs + [(b, a) for a, b in pairs])
        for value, pairs in zip((near_sent, far_sent), swaps)
    )
    saved_own, *saved = home_slots(bwd_in, routing, group)
    saved_rows = [saved_own, *sent(saved)]
    section_x, section_g, x_own, g_own, *streams = stream_slots(
        routing, near_sent, near, far, group, last
    )
    stream_rows = sent(streams)

    def summed(own, arrived):
        total = own.astype(F32)
        for value in arrived:
            total = total + value.astype(F32)
        return total

    back_parts = in_partials(saved_rows, gate, up, group)
    back_sent = sent(back_parts[1:])
    stream_rows = after(stream_rows, back_parts)
    x_parts = in_partials([x_own, *stream_rows], gate, up, group, 0)
    x_sent = sent(x_parts[1:])
    g_parts = grad_partials([after(g_own, x_parts), *stream_rows], down, group, 1)
    g_sent = sent(g_parts[1:])

    back_sent = after(back_sent, g_parts)
    back = summed(back_parts[0], back_sent)
    x_sent = after(x_sent, back)
    ahead = summed(x_parts[0], x_sent)
    hidden = (jax.nn.silu(ahead[0]) * ahead[1]).astype(BF16)
    hidden_sent = sent([hidden] * (group - 1))

    g_sent = after(g_sent, hidden)
    grad_hidden = summed(g_parts[0], g_sent)
    sig = jax.nn.sigmoid(back[0])
    grad_gate = grad_hidden * back[1] * sig * (1.0 + back[0] * (1.0 - sig))
    grad_up = grad_hidden * (back[0] * sig)
    cut = grad_up.shape[1] // 4
    begun = jnp.concatenate([grad_gate, grad_up[:, :cut]], axis=1).astype(BF16)
    rest = (after(grad_hidden, begun) * (back[0] * sig))[:, cut:].astype(BF16)
    begun_sent = sent([begun] * (group - 1))
    rest_sent = sent([rest] * (group - 1))

    def returned(blocks):
        rows = sent(blocks[1:])
        return [blocks[0], *rows[: group - 1]], rows[group - 1 :]

    fwd_pick, bwd_pick, fwd_weights, bwd_weights = picks_of(
        after(routing, hidden), fwd_gates, bwd_gates, group
    )
    hidden_sent = after(hidden_sent, fwd_pick)
    fwd_rows = down_rows([hidden, *hidden_sent], down)
    fwd_same, fwd_other = returned(fwd_rows)
    total = back_first([begun, *after(begun_sent, fwd_rows)], gate, up)
    bwd_same, bwd_other = returned(back_last([rest, *after(rest_sent, total)], up, total))
    fwd_out = combine(fwd_pick, fwd_weights, section_x, fwd_same, fwd_other)
    bwd_out = combine(bwd_pick, bwd_weights, section_g, bwd_same, bwd_other)
    return (fwd_out[None], bwd_out[None])


def solution(mesh):
    spec = P("pipe", "expert", None)
    return jax.shard_map(
        body,
        mesh=mesh,
        in_specs=(spec,) * 5 + (P("pipe", None, "expert"),) + (spec,) * 4,
        out_specs=(spec, spec),
        check_vma=False,
    )
```
